512 devices in a mesh: dp: 16 (over z_lo, x), zero: 32 (over y, z_hi, core).
Axes of the slice: x: 4, y: 8, z: 8 (z_hi: 2, z_lo: 4; z = z_hi * 4 + z_lo), core: 2. Of those that a mesh axis runs over, the one named last changes fastest.
Arguments:
- gate_up: bfloat16 [2, 4096, 14336], P(None, 'dp', 'zero'), may hold values from -6 to 6
- cot_mean: bfloat16 [4096, 4096], P('dp', 'zero'), may hold values from -6 to 6
- label_rows: bfloat16 [64, 4096], P(None, 'dp'), may hold values from -6 to 6
- true_labels: int32 [4096], P('dp'), may hold values from 0 to 63
- sampled_labels: int32 [4096], P('dp'), may hold values from 0 to 63
- weight: bfloat16 [14336, 4096], P('zero', 'dp'), may hold values from -4 to 4
- moment: bfloat16 [14336, 4096], P('zero', 'dp'), may hold values from -0.29882812 to 0.29882812
- curvature: bfloat16 [14336, 4096], P('zero', 'dp'), may hold values from 0.0099487305 to 1
- bits: int32 [14336, 4096], P('zero', 'dp'), may hold values from 0 to 16383
Outputs:
- new_weight: bfloat16 [14336, 4096], P('zero')
- new_moment: bfloat16 [14336, 4096], P('zero', 'dp')
- new_curvature: bfloat16 [14336, 4096], P('zero', 'dp')
The draws below stay inside these ranges and needn't reach their ends.
All inputs are finite; a program needn't handle non-finite values.
Results may differ from the reference program's by a relative error of at most 0.014.
Values may be sent and summed in bfloat16 or wider, within the bound.
A program may use at most 64 MiB of HBM per device.

```python
import math
import jax
import jax.numpy as jnp
import numpy as np
from jax import lax

D = 4096
HB = 14336
TOK_DEV = 256
CAND = 64
TOKENS = 4096
N_DP = 16


def set_ends(result, own_key, smallest, high):
    spot = [jax.random.randint(jax.random.fold_in(own_key, axis), (), 0, length) for axis, length in enumerate(result.shape)]
    widest = result.shape.index(max(result.shape))
    beside = spot[:widest] + [(spot[widest] + 1) % result.shape[widest]] + spot[widest + 1:]
    return result.at[tuple(spot)].set(smallest).at[tuple(beside)].set(high)


def strengthened(entries, stream_key, source, target, blocks, factor):
    def block_of(dim):
        return (jnp.arange(entries.shape[dim]) // (entries.shape[dim] // blocks)).reshape((-1,) + (1,) * (entries.ndim - 1 - dim))

    near = jax.random.permutation(stream_key, blocks)[block_of(target)]
    other_side = (block_of(target) + blocks // 2) % blocks
    return jnp.where((block_of(source) == near) | (block_of(source) == other_side), factor * entries, entries)


def block_scale(rng, extent, cuts, smallest, high):
    factor_of = 1.0
    for axis_at, blocks in cuts:
        draws = jax.random.uniform(jax.random.fold_in(jax.random.fold_in(rng, 6), axis_at), (blocks,), jnp.float32, smallest / len(cuts), high / len(cuts))
        factor_of = factor_of * jnp.repeat(jnp.exp(draws), extent[axis_at] // blocks).reshape((-1,) + (1,) * (len(extent) - 1 - axis_at))
    return factor_of


def rank_table(number_of, slope):
    portions = [(1 << 20) // math.isqrt(grade ** slope) + 1 for grade in range(1, number_of + 1)]
    spread = 1 + sum(portions) // (1 << 30)
    return np.cumsum(np.array([max(1, weight // spread) for weight in portions]))


def ranked_ids(stream_key, dims, number_of, lean):
    table = rank_table(number_of, lean)
    ticket = jax.random.randint(jax.random.fold_in(stream_key, 1), dims, 0, int(table[number_of - 1]))
    rank = jnp.searchsorted(jnp.asarray(table, jnp.int32), ticket, side="right")
    return jax.random.permutation(jax.random.fold_in(stream_key, 2), number_of)[rank].astype(jnp.int32)


def normal_values(key, extent, scale, bound, split=(), kind=jnp.bfloat16):
    factor_of = block_scale(key, extent, split, -0.22, 0.18) if split else 1.0
    drawn = jax.random.normal(key, extent, jnp.float32) * scale * factor_of
    return jnp.minimum(jnp.maximum(drawn, -bound), bound).astype(kind)


def noise_with(rng, dims, width, reach, split, heavy, held_as=jnp.bfloat16):
    array = width * jax.random.normal(rng, dims, jnp.float32)
    if split:
        array = array * block_scale(rng, dims, split, -0.22, 0.18)
    return jnp.clip(strengthened(array, jax.random.fold_in(rng, 3), *heavy), -reach, reach).astype(held_as)


def setup_inputs(seed: int = 0) -> dict:
    splits = jax.random.split(jax.random.key(seed), 10)
    return {
        "gate_up": normal_values(splits[0], (2, TOKENS, HB), 1.0, 6.0, ((1, 16), (2, 32))),
        "cot_mean": noise_with(splits[1], (TOKENS, D), 1.0, 6.0, ((0, 16), (1, 32)), (0, 1, 32, 2.75)),
        "label_rows": normal_values(splits[2], (CAND, D), 1.0, 6.0, ((1, 16),)),
        "true_labels": set_ends(ranked_ids(splits[3], (TOKENS,), CAND, 2), jax.random.fold_in(splits[3], 3), 0, CAND - 1).astype(jnp.int32),
        "sampled_labels": set_ends(jax.random.randint(splits[4], (TOKENS,), 0, CAND), jax.random.fold_in(splits[4], 1), 0, CAND - 1).astype(jnp.int32),
        "weight": normal_values(splits[5], (HB, D), 1.0, 4.0, ((0, 32), (1, 16))),
        "moment": normal_values(splits[6], (HB, D), 0.05, 0.29882812, ((0, 32), (1, 16))),
        "curvature": jnp.clip(jnp.exp(math.log(1.0) - 4.61031033 * jax.random.uniform(splits[7], (HB, D), jnp.float32) ** block_scale(splits[7], (HB, D), ((0, 32), (1, 16)), -0.2, 0.2)), 0.0099487305, 1.0).astype(jnp.bfloat16),
        "bits": set_ends(jax.random.randint(splits[8], (HB, D), 0, 16384), jax.random.fold_in(splits[8], 1), 0, 16383).astype(jnp.int32),
    }


beta_one = 0.965
beta_two = 0.99
gamma_rate = 0.5
learn_rate = 0.05
decay_rate = 0.1

def dither(value, noise):
    return (value * (1.0 + (noise - 0.5) / 8.0)).astype(jnp.bfloat16)

def reference(gate_up, cot_mean, label_rows, true_labels, sampled_labels, weight, moment, curvature, bits):
    gate_part = gate_up[0].astype(jnp.float32)
    up_part = gate_up[1].astype(jnp.float32)
    hidden = (jax.nn.silu(gate_part) * up_part).astype(jnp.bfloat16)

    def add_group(index, total):
        start = (index * TOK_DEV).astype(jnp.int32)
        rows_h = lax.dynamic_slice_in_dim(hidden, start, TOK_DEV, 0)
        rows_c = lax.dynamic_slice_in_dim(cot_mean, start, TOK_DEV, 0)
        piece = jnp.dot(rows_h.T, rows_c, preferred_element_type=jnp.float32).astype(jnp.bfloat16)
        return total + lax.optimization_barrier(piece).astype(jnp.float32)
    grad_common = lax.fori_loop(0, N_DP, add_group, jnp.zeros((HB, D), jnp.float32))
    classes = jnp.arange(CAND, dtype=jnp.int32)
    hot_true = (true_labels[:, None] == classes[None, :]).astype(jnp.bfloat16)
    hot_sampled = (sampled_labels[:, None] == classes[None, :]).astype(jnp.bfloat16)
    label_true = jnp.dot(hidden.T, hot_true, preferred_element_type=jnp.float32)
    label_sampled = jnp.dot(hidden.T, hot_sampled, preferred_element_type=jnp.float32)
    label_wide = label_rows.astype(jnp.float32)
    factor = 1.0 / math.sqrt(TOKENS)
    grad_true = (grad_common - jnp.dot(label_true, label_wide, precision=lax.Precision.HIGHEST)) * factor
    grad_sampled = (grad_common - jnp.dot(label_sampled, label_wide, precision=lax.Precision.HIGHEST)) * factor
    low_bits = bits % 128
    high_bits = bits // 128
    noise_one = (low_bits.astype(jnp.float32) + 0.5) / 128.0
    noise_two = (high_bits.astype(jnp.float32) + 0.5) / 128.0
    noise_three = (((3 * low_bits + 5 * high_bits) % 128).astype(jnp.float32) + 0.5) / 128.0
    new_moment = dither(beta_one * moment.astype(jnp.float32) + (1.0 - beta_one) * grad_true, noise_one)
    new_curvature = dither(beta_two * curvature.astype(jnp.float32) + (1.0 - beta_two) * grad_sampled * grad_sampled, noise_two)
    ratio = jnp.clip(new_moment.astype(jnp.float32) / (gamma_rate * new_curvature.astype(jnp.float32)), -1.0, 1.0)
    shrunk = weight.astype(jnp.float32) * (1.0 - learn_rate * decay_rate) - learn_rate * ratio
    new_weight = dither(shrunk, noise_three)
    return (new_weight, new_moment, new_curvature)
```

```python
import math

import jax
import jax.numpy as jnp
from jax import lax
from jax.experimental import pallas as pl
from jax.experimental.pallas import tpu as pltpu
from jax.sharding import PartitionSpec as P

beta_one = 0.965
beta_two = 0.99
gamma_rate = 0.5
learn_rate = 0.05
decay_rate = 0.1

NX, NL, NY, NH, NC = 4, 4, 8, 2, 2
NZ = NH * NL
ROWS, TOK, COLS, HALF, CAND = 448, 256, 256, 128, 64
PARTS = 4
STEP = ROWS // PARTS
TOP = ROWS // 2
BF16, F32, I32 = jnp.bfloat16, jnp.float32, jnp.int32


def device(x, y, zh, zl, core):
    return (zl * NX + x, (y * NH + zh) * NC + core)


def remote(src, dst, send, recv, to):
    return pltpu.make_async_remote_copy(
        src, dst, send, recv, device_id=to, device_id_type=pl.DeviceIdType.MESH
    )


def arrived(dst, sem):
    pltpu.make_async_copy(dst, dst, sem).wait()


def step_kernel(
    gate_in, cot_in, rows_in, true_in, sampled_in, weight_in, moment_in, curv_in, bits_in,
    wout, mout, cout,
    gate_v, cot_v, rows_v, true_v, sampled_v, weight_v, moment_v, curv_v, bits_v,
    hid, labs, cot, part, own_part, first, second, lab_sum, wide_rows, corr,
    load_sem, own_cot_send, cot_recv, chain_send, sib_send, sib_recv,
    hid_send, hid_recv, labs_send, labs_recv, sum_send, sum_recv,
    first_send, first_recv, second_send, second_recv, out_send, out_recv,
):
    dp = lax.axis_index("dp")
    zero = lax.axis_index("zero")
    x, zl = dp % NX, dp // NX
    core, zh, y = zero % NC, (zero // NC) % NH, zero // (NC * NH)
    z = zh * NL + zl
    xr, xo, xl = (x + 1) % NX, (x + 2) % NX, (x + 3) % NX
    right, across, left = [device(v, y, zh, zl, core) for v in (xr, xo, xl)]
    y_up, y_down = [device(x, (y + d) % NY, zh, zl, core) for d in (1, NY - 1)]
    sibling = device(x, y, zh, zl, 1 - core)
    line = [(zl + k) % NL for k in range(1, NL)]
    line_dev = [device(x, y, zh, v, core) for v in line]

    loads = [
        pltpu.make_async_copy(src, dst, load_sem.at[n])
        for n, (src, dst) in enumerate([
            (cot_in, cot_v), (gate_in, gate_v), (true_in, true_v), (sampled_in, sampled_v),
            (rows_in, rows_v), (moment_in, moment_v), (curv_in, curv_v), (bits_in, bits_v),
            (weight_in, weight_v),
        ])
    ]
    for load in loads:
        load.start()

    barrier = pltpu.get_barrier_semaphore()
    partners = [right, across, left, y_up, y_down, sibling]
    for k in range(1, NZ):
        other = (z + k) % NZ
        partners.append(device(x, y, other // NL, other % NL, core))
    for partner in partners:
        pl.semaphore_signal(
            barrier, inc=1, device_id=partner, device_id_type=pl.DeviceIdType.MESH
        )
    loads[0].wait()
    pl.semaphore_wait(barrier, len(partners))

    row = y // 2
    own_slot = cot.at[(y % 2) * 2 + zh, core, zl]

    def own_copy(h):
        return remote(
            cot_v, own_slot, own_cot_send.at[h], cot_recv.at[y % 2, z],
            device(x, y, h, row, core),
        )

    for h in range(NH):
        @pl.when(jnp.logical_or(zl != row, zh != h))
        def _():
            own_copy(h).start()

    @pl.when(zl == row)
    def _():
        pltpu.make_async_copy(cot_v, own_slot, cot_recv.at[y % 2, z]).start()

    loads[1].wait()
    gate = gate_v[0].astype(F32)
    up = gate_v[1].astype(F32)
    hid[zl] = (jax.nn.silu(gate) * up).astype(BF16)
    hid_copies = [
        remote(hid.at[zl], hid.at[zl], hid_send.at[k], hid_recv.at[zl], line_dev[k])
        for k in range(NL - 1)
    ]
    for copy in hid_copies:
        copy.start()
    loads[2].wait()
    loads[3].wait()
    labs[zl, 0:1] = true_v[...]
    labs[zl, 1:2] = sampled_v[...]
    labs[zl, 2:8] = jnp.zeros((6, TOK), I32)
    labs_copies = [
        remote(labs.at[zl], labs.at[zl], labs_send.at[k], labs_recv.at[zl], line_dev[k])
        for k in range(NL - 1)
    ]
    for copy in labs_copies:
        copy.start()

    place = (y - 2 * zl + NY) % NY
    lag = (
        jnp.where(place == 1, 1, (NY - place) % NY),
        jnp.where(place == 0, 1, place - 1),
    )
    goes_up = (place == 0, jnp.logical_and(place >= 1, place <= 6))
    goes_down = (jnp.logical_or(place == 0, place >= 3), place == 1)

    def slot_of(yb, k, half):
        return cot.at[yb * 2 + k // NL, half, k % NL]

    def chain_copies(yb, k):
        slot = slot_of(yb, k, core)
        return (
            remote(slot, slot, chain_send.at[yb, k, 0], cot_recv.at[yb, k], y_up),
            remote(slot, slot, chain_send.at[yb, k, 1], cot_recv.at[yb, k], y_down),
            remote(slot, slot, sib_send.at[yb, k], sib_recv.at[yb, k], sibling),
        )

    def chain_step(t, carry):
        for yb in (0, 1):
            k = t - lag[yb]

            @pl.when(jnp.logical_and(k >= 0, k < NZ))
            def _():
                arrived(slot_of(yb, k, core), cot_recv.at[yb, k])
                up_copy, down_copy, sib_copy = chain_copies(yb, k)

                @pl.when(goes_up[yb])
                def _():
                    up_copy.start()

                @pl.when(goes_down[yb])
                def _():
                    down_copy.start()

                sib_copy.start()

        return carry

    lax.fori_loop(0, NZ + 6, chain_step, 0)

    for v in line:
        arrived(hid.at[v], hid_recv.at[v])
        arrived(labs.at[v], labs_recv.at[v])
    classes = lax.broadcasted_iota(I32, (CAND, TOK), 0)
    total = jnp.zeros((ROWS, 2 * CAND), F32)
    for v in range(NL):
        lab = labs[v]
        hot = jnp.concatenate(
            [(classes == lab[n:n + 1]).astype(F32) for n in (0, 1)], axis=0
        ).astype(BF16)
        total += lax.dot_general(
            hid[v], hot, (((1,), (1,)), ((), ())), preferred_element_type=F32
        )
    lab_sum[x] = total.astype(BF16)
    sum_copies = [
        remote(lab_sum.at[x], lab_sum.at[x], sum_send.at[n], sum_recv.at[x], to)
        for n, to in enumerate((right, across, left))
    ]

    def wait_sibling(k, carry):
        for yb in (0, 1):
            arrived(slot_of(yb, k, 1 - core), sib_recv.at[yb, k])
        return carry

    lax.fori_loop(0, NZ, wait_sibling, 0)

    def partial_of(owner):
        acc = jnp.zeros((ROWS, COLS), F32)
        for v in range(NL):
            wide = jnp.concatenate([cot[owner, 0, v], cot[owner, 1, v]], axis=1)
            acc += jnp.dot(hid[v], wide, preferred_element_type=F32)
        return acc

    part[2] = partial_of(xo).astype(BF16)
    first_copies = [
        remote(part.at[2, pl.ds(0, TOP)], first.at[0], first_send.at[0], first_recv.at[0], right),
        remote(part.at[2, pl.ds(TOP, TOP)], first.at[1], first_send.at[1], first_recv.at[1], left),
    ]
    for copy in first_copies:
        copy.start()
    for copy in sum_copies:
        copy.start()
    part[1] = partial_of(xr).astype(BF16)
    part[3] = partial_of(xl).astype(BF16)

    def second_copies(q):
        rows = pl.ds(q * STEP, STEP)
        return (
            remote(part.at[1, rows], second.at[0, rows], second_send.at[0, q],
                   second_recv.at[0, q], right),
            remote(part.at[3, rows], second.at[1, rows], second_send.at[1, q],
                   second_recv.at[1, q], left),
        )

    half = PARTS // 2
    for q in range(half):
        second_copies(half + q)[0].start()
        second_copies(q)[1].start()
    arrived(first.at[0], first_recv.at[0])
    arrived(first.at[1], first_recv.at[1])
    for q in range(half):
        rows = pl.ds(q * STEP, STEP)
        low = pl.ds(TOP + q * STEP, STEP)
        part[1, rows] = (part[1, rows].astype(F32) + first[0, rows].astype(F32)).astype(BF16)
        second_copies(q)[0].start()
        part[3, low] = (part[3, low].astype(F32) + first[1, rows].astype(F32)).astype(BF16)
        second_copies(half + q)[1].start()
    own_part[...] = partial_of(x)

    loads[4].wait()
    blank = jnp.zeros((CAND, COLS), BF16)
    wide_rows[0:CAND, 0:COLS] = rows_v[...]
    wide_rows[0:CAND, COLS:2 * COLS] = blank
    wide_rows[CAND:2 * CAND, 0:COLS] = blank
    wide_rows[CAND:2 * CAND, COLS:2 * COLS] = rows_v[...]
    for v in (xl, xr, xo):
        arrived(lab_sum.at[v], sum_recv.at[v])
    rest = jnp.zeros((ROWS, 2 * CAND), F32)
    for v in range(NX):
        rest += lab_sum[v].astype(F32)
    terms = []
    for _ in range(3):
        term = rest.astype(BF16)
        terms.append(term)
        rest = rest - term.astype(F32)
    spread = wide_rows[...]
    corr[...] = (
        jnp.dot(terms[2], spread, preferred_element_type=F32)
        + jnp.dot(terms[1], spread, preferred_element_type=F32)
    ) + jnp.dot(terms[0], spread, preferred_element_type=F32)

    for n in (5, 6, 7, 8):
        loads[n].wait()
    factor = 1.0 / math.sqrt(TOK * NX * NL)

    def out_copy(q, index, n, to):
        piece = wout.at[index, pl.ds(q * STEP, STEP)]
        return remote(piece, piece, out_send.at[q, n], out_recv.at[q, index], to)

    def own_sends(q):
        return [out_copy(q, dp, n, to) for n, to in enumerate(line_dev + [right, left])]

    def line_sends(q):
        return [
            out_copy(q, v * NX + x, 5 + 2 * m + d, to)
            for m, v in enumerate(line) for d, to in enumerate((right, left))
        ]

    def forwards(q):
        order = [zl] + line
        return [
            out_copy(q, v * NX + (xl if m < 2 else xr), 11 + m, right if m < 2 else left)
            for m, v in enumerate(order)
        ]

    def out_arrived(q, index):
        arrived(wout.at[index, pl.ds(q * STEP, STEP)], out_recv.at[q, index])

    def finish(q, carry):
        rows = pl.ds(pl.multiple_of(q * STEP, STEP), STEP)
        arrived(second.at[0, rows], second_recv.at[0, q])
        arrived(second.at[1, rows], second_recv.at[1, q])
        common = (
            own_part[rows, :] + second[0, rows, :].astype(F32) + second[1, rows, :].astype(F32)
        )
        grad_true = (common - corr[rows, 0:COLS]) * factor
        grad_sampled = (common - corr[rows, COLS:2 * COLS]) * factor
        drawn = bits_v[rows, :]
        low = jnp.bitwise_and(drawn, 127)
        high = jnp.right_shift(drawn, 7)
        mixed = jnp.bitwise_and(3 * low + 5 * high, 127)

        def dither(value, noise):
            scale = (noise.astype(F32) + 960.5) * (1.0 / 1024.0)
            return (value * scale).astype(BF16)

        new_moment = dither(
            beta_one * moment_v[rows, :].astype(F32) + (1.0 - beta_one) * grad_true, low
        )
        new_curv = dither(
            beta_two * curv_v[rows, :].astype(F32)
            + (1.0 - beta_two) * grad_sampled * grad_sampled,
            high,
        )
        ratio = jnp.clip(
            new_moment.astype(F32) / (gamma_rate * new_curv.astype(F32)), -1.0, 1.0
        )
        shrunk = (
            weight_v[rows, :].astype(F32) * (1.0 - learn_rate * decay_rate) - learn_rate * ratio
        )
        mout[rows, :] = new_moment
        cout[rows, :] = new_curv
        wout[dp, rows, :] = dither(shrunk, mixed)
        for copy in own_sends(q):
            copy.start()
        return carry

    lax.fori_loop(0, PARTS, finish, 0)

    def pass_line(q):
        for m, v in enumerate(line):
            out_arrived(q, v * NX + x)
            line_sends(q)[2 * m].start()
            line_sends(q)[2 * m + 1].start()

    def pass_ring(q):
        copies = forwards(q)
        for m, v in enumerate([zl] + line):
            out_arrived(q, v * NX + xl)
            out_arrived(q, v * NX + xr)
            copies[m].start()

    def spread_step(t, carry):
        @pl.when(t < PARTS)
        def _():
            pass_line(t)

        @pl.when(t > 0)
        def _():
            pass_ring(t - 1)

        return carry

    lax.fori_loop(0, PARTS + 1, spread_step, 0)

    def last_step(q, carry):
        for v in [zl] + line:
            out_arrived(q, v * NX + xo)
        for copy in own_sends(q) + line_sends(q) + forwards(q):
            copy.wait_send()
        for copy in second_copies(q):
            copy.wait_send()
        return carry

    lax.fori_loop(0, PARTS, last_step, 0)

    for h in range(NH):
        @pl.when(jnp.logical_or(zl != row, zh != h))
        def _():
            own_copy(h).wait_send()

    for copy in hid_copies + labs_copies + sum_copies + first_copies:
        copy.wait_send()

    def drain_chain(k, carry):
        for yb in (0, 1):
            up_copy, down_copy, sib_copy = chain_copies(yb, k)

            @pl.when(goes_up[yb])
            def _():
                up_copy.wait_send()

            @pl.when(goes_down[yb])
            def _():
                down_copy.wait_send()

            sib_copy.wait_send()

        return carry

    lax.fori_loop(0, NZ, drain_chain, 0)


def place_kernel(wide, moment, curv, wide_out, moment_out, curv_out, sem):
    copies = [
        pltpu.make_async_copy(
            wide.at[n], wide_out.at[:, pl.ds(n * COLS, COLS)], sem.at[n]
        )
        for n in range(NX * NL)
    ]
    copies.append(pltpu.make_async_copy(moment, moment_out, sem.at[NX * NL]))
    copies.append(pltpu.make_async_copy(curv, curv_out, sem.at[NX * NL + 1]))
    for copy in copies:
        copy.start()
    for copy in copies:
        copy.wait()


def on_device(
    gate_up, cot_mean, label_rows, true_labels, sampled_labels, weight, moment, curvature, bits
):
    dma = pltpu.SemaphoreType.DMA
    groups = NX * NL
    anywhere = pl.BlockSpec(memory_space=pl.ANY)
    in_vmem = pl.BlockSpec(memory_space=pltpu.VMEM)
    state = (ROWS, COLS)
    pieces, new_moment, new_curv = pl.pallas_call(
        step_kernel,
        out_shape=[
            pltpu.VMEM((groups, ROWS, COLS), BF16),
            pltpu.VMEM(state, BF16),
            pltpu.VMEM(state, BF16),
        ],
        in_specs=[anywhere] * 9,
        out_specs=[in_vmem] * 3,
        scratch_shapes=[
            pltpu.VMEM((2, ROWS, TOK), BF16),
            pltpu.VMEM((TOK, HALF), BF16),
            pltpu.VMEM((CAND, COLS), BF16),
            pltpu.VMEM((1, TOK), I32),
            pltpu.VMEM((1, TOK), I32),
            pltpu.VMEM(state, BF16),
            pltpu.VMEM(state, BF16),
            pltpu.VMEM(state, BF16),
            pltpu.VMEM(state, I32),
            pltpu.VMEM((NL, ROWS, TOK), BF16),
            pltpu.VMEM((NL, 8, TOK), I32),
            pltpu.VMEM((NX, NC, NL, TOK, HALF), BF16),
            pltpu.VMEM((NX, ROWS, COLS), BF16),
            pltpu.VMEM(state, F32),
            pltpu.VMEM((2, TOP, COLS), BF16),
            pltpu.VMEM((2, ROWS, COLS), BF16),
            pltpu.VMEM((NX, ROWS, 2 * CAND), BF16),
            pltpu.VMEM((2 * CAND, 2 * COLS), BF16),
            pltpu.VMEM((ROWS, 2 * COLS), F32),
            dma((9,)),
            dma((NH,)),
            dma((2, NZ)),
            dma((2, NZ, 2)),
            dma((2, NZ)),
            dma((2, NZ)),
            dma((NL - 1,)),
            dma((NL,)),
            dma((NL - 1,)),
            dma((NL,)),
            dma((3,)),
            dma((NX,)),
            dma((2,)),
            dma((2,)),
            dma((2, PARTS)),
            dma((2, PARTS)),
            dma((PARTS, 15)),
            dma((PARTS, groups)),
        ],
        compiler_params=pltpu.CompilerParams(
            collective_id=0, has_side_effects=True, vmem_limit_bytes=32 * 1024 * 1024
        ),
        cost_estimate=pl.CostEstimate(
            flops=1_000_000_000, bytes_accessed=6_000_000, transcendentals=114_688
        ),
        name="sophia_step",
    )(
        jnp.swapaxes(gate_up, 1, 2), cot_mean, label_rows,
        true_labels.reshape(1, TOK), sampled_labels.reshape(1, TOK),
        weight, moment, curvature, bits,
    )
    return pl.pallas_call(
        place_kernel,
        out_shape=[
            jax.ShapeDtypeStruct((ROWS, groups * COLS), BF16),
            jax.ShapeDtypeStruct(state, BF16),
            jax.ShapeDtypeStruct(state, BF16),
        ],
        in_specs=[in_vmem] * 3,
        out_specs=[anywhere] * 3,
        scratch_shapes=[dma((groups + 2,))],
        name="place",
    )(pieces, new_moment, new_curv)


def solution(mesh):
    in_specs = (
        P(None, "dp", "zero"),
        P("dp", "zero"),
        P(None, "dp"),
        P("dp"),
        P("dp"),
        P("zero", "dp"),
        P("zero", "dp"),
        P("zero", "dp"),
        P("zero", "dp"),
    )
    out_specs = (P("zero", None), P("zero", "dp"), P("zero", "dp"))
    return jax.shard_map(
        on_device, mesh=mesh, in_specs=in_specs, out_specs=out_specs, check_vma=False
    )
```

```python
import math

import jax
import jax.numpy as jnp
from jax import lax
from jax.experimental import pallas as pl
from jax.experimental.pallas import tpu as pltpu
from jax.sharding import PartitionSpec as P

beta_one = 0.965
beta_two = 0.99
gamma_rate = 0.5
learn_rate = 0.05
decay_rate = 0.1

NX, NL, NY, NH, NC = 4, 4, 8, 2, 2
NZ = NH * NL
ROWS, TOK, COLS, HALF, CAND = 448, 256, 256, 128, 64
PARTS = 4
SUB, LAG = 1, 3
BLOCKS = NZ * SUB
FINE = TOK // SUB
STEP = ROWS // PARTS
TOP = ROWS // 2
BF16, F32, I32 = jnp.bfloat16, jnp.float32, jnp.int32


def device(x, y, zh, zl, core):
    return (zl * NX + x, (y * NH + zh) * NC + core)


def remote(src, dst, send, recv, to):
    return pltpu.make_async_remote_copy(
        src, dst, send, recv, device_id=to, device_id_type=pl.DeviceIdType.MESH
    )


def arrived(dst, sem):
    pltpu.make_async_copy(dst, dst, sem).wait()


def step_kernel(
    gate_in, cot_in, rows_in, true_in, sampled_in, weight_in, moment_in, curv_in, bits_in,
    wout, mout, cout,
    gate_v, cot_v, rows_v, true_v, sampled_v, weight_v, moment_v, curv_v, bits_v,
    hid, labs, cot, part, own_part, first, second, lab_sum, wide_rows, corr,
    load_sem, own_cot_send, cot_recv, chain_send, sib_send, sib_recv,
    hid_send, hid_recv, labs_send, labs_recv, sum_send, sum_recv,
    first_send, first_recv, second_send, second_recv, out_send, out_recv,
):
    dp = lax.axis_index("dp")
    zero = lax.axis_index("zero")
    x, zl = dp % NX, dp // NX
    core, zh, y = zero % NC, (zero // NC) % NH, zero // (NC * NH)
    z = zh * NL + zl
    xr, xo, xl = (x + 1) % NX, (x + 2) % NX, (x + 3) % NX
    right, across, left = [device(v, y, zh, zl, core) for v in (xr, xo, xl)]
    y_up, y_down = [device(x, (y + d) % NY, zh, zl, core) for d in (1, NY - 1)]
    sibling = device(x, y, zh, zl, 1 - core)
    line = [(zl + k) % NL for k in range(1, NL)]
    line_dev = [device(x, y, zh, v, core) for v in line]

    loads = [
        pltpu.make_async_copy(src, dst, load_sem.at[n])
        for n, (src, dst) in enumerate([
            (cot_in, cot_v), (gate_in, gate_v), (true_in, true_v), (sampled_in, sampled_v),
            (rows_in, rows_v), (moment_in, moment_v), (curv_in, curv_v), (bits_in, bits_v),
            (weight_in, weight_v),
        ])
    ]
    for load in loads:
        load.start()

    barrier = pltpu.get_barrier_semaphore()
    partners = [right, across, left, y_up, y_down, sibling]
    y_far = (y + NY // 2) % NY
    for k in range(NZ):
        other = (z + k) % NZ
        if k:
            partners.append(device(x, y, other // NL, other % NL, core))
        partners.append(device(x, y_far, other // NL, other % NL, core))
    for partner in partners:
        pl.semaphore_signal(
            barrier, inc=1, device_id=partner, device_id_type=pl.DeviceIdType.MESH
        )
    loads[0].wait()
    pl.semaphore_wait(barrier, len(partners))

    row = y // 2
    own_slot = cot.at[(y % 2) * 2 + zh, core, zl]

    def fine_of(ref, n):
        return ref.at[pl.ds(n * FINE, FINE)]

    def own_copy(far, h, n):
        return remote(
            fine_of(cot_v, n), fine_of(own_slot, n), own_cot_send.at[far, h, n],
            cot_recv.at[y % 2, z, n], device(x, (y, y_far)[far], h, row, core),
        )

    for h in range(NH):
        @pl.when(jnp.logical_or(zl != row, zh != h))
        def _():
            for n in range(SUB):
                own_copy(0, h, n).start()

        for n in range(SUB):
            own_copy(1, h, n).start()

    @pl.when(zl == row)
    def _():
        for n in range(SUB):
            pltpu.make_async_copy(
                fine_of(cot_v, n), fine_of(own_slot, n), cot_recv.at[y % 2, z, n]
            ).start()

    loads[1].wait()
    gate = gate_v[0].astype(F32)
    up = gate_v[1].astype(F32)
    hid[zl] = (jax.nn.silu(gate) * up).astype(BF16)
    hid_copies = [
        remote(hid.at[zl], hid.at[zl], hid_send.at[k], hid_recv.at[zl], line_dev[k])
        for k in range(NL - 1)
    ]
    for copy in hid_copies:
        copy.start()
    loads[2].wait()
    loads[3].wait()
    labs[zl, 0:1] = true_v[...]
    labs[zl, 1:2] = sampled_v[...]
    labs[zl, 2:8] = jnp.zeros((6, TOK), I32)
    labs_copies = [
        remote(labs.at[zl], labs.at[zl], labs_send.at[k], labs_recv.at[zl], line_dev[k])
        for k in range(NL - 1)
    ]
    for copy in labs_copies:
        copy.start()

    place = (y - 2 * zl + NY) % (NY // 2)
    lag = (
        jnp.where(place == 1, 1, (4 - place) % 4),
        jnp.where(place == 0, 1, place - 1),
    )
    goes_up = (place == 0, jnp.logical_or(place == 1, place == 2))
    goes_down = (jnp.logical_or(place == 0, place == 3), place == 1)

    def slot_of(yb, k, half):
        step, n = k // SUB, k % SUB
        src = jnp.where(step % 2 == 1, z + (step + 1) // 2, z + NZ - step // 2) % NZ
        return cot.at[yb * 2 + src // NL, half, src % NL, pl.ds(n * FINE, FINE)], src, n

    def chain_copies(yb, k):
        slot, src, n = slot_of(yb, k, core)
        return (
            remote(slot, slot, chain_send.at[yb, k, 0], cot_recv.at[yb, src, n], y_up),
            remote(slot, slot, chain_send.at[yb, k, 1], cot_recv.at[yb, src, n], y_down),
            remote(slot, slot, sib_send.at[yb, k], sib_recv.at[yb, k], sibling),
        )

    def chain_step(t, carry):
        for yb in (0, 1):
            k = t - LAG * lag[yb]

            @pl.when(jnp.logical_and(k >= 0, k < BLOCKS))
            def _():
                slot, src, n = slot_of(yb, k, core)
                arrived(slot, cot_recv.at[yb, src, n])
                up_copy, down_copy, sib_copy = chain_copies(yb, k)

                @pl.when(goes_up[yb])
                def _():
                    up_copy.start()

                @pl.when(goes_down[yb])
                def _():
                    down_copy.start()

                sib_copy.start()

        return carry

    lax.fori_loop(0, BLOCKS + 2 * LAG, chain_step, 0)

    for v in line:
        arrived(hid.at[v], hid_recv.at[v])
        arrived(labs.at[v], labs_recv.at[v])
    classes = lax.broadcasted_iota(I32, (CAND, TOK), 0)
    total = jnp.zeros((ROWS, 2 * CAND), F32)
    for v in range(NL):
        lab = labs[v]
        hot = jnp.concatenate(
            [(classes == lab[n:n + 1]).astype(F32) for n in (0, 1)], axis=0
        ).astype(BF16)
        total += lax.dot_general(
            hid[v], hot, (((1,), (1,)), ((), ())), preferred_element_type=F32
        )
    lab_sum[x] = total.astype(BF16)
    sum_copies = [
        remote(lab_sum.at[x], lab_sum.at[x], sum_send.at[n], sum_recv.at[x], to)
        for n, to in enumerate((right, across, left))
    ]

    def wait_sibling(k, carry):
        for yb in (0, 1):
            arrived(slot_of(yb, k, 1 - core)[0], sib_recv.at[yb, k])
        return carry

    lax.fori_loop(0, BLOCKS, wait_sibling, 0)

    def partial_of(owner):
        acc = jnp.zeros((ROWS, COLS), F32)
        for v in range(NL):
            wide = jnp.concatenate([cot[owner, 0, v], cot[owner, 1, v]], axis=1)
            acc += jnp.dot(hid[v], wide, preferred_element_type=F32)
        return acc

    part[2] = partial_of(xo).astype(BF16)
    first_copies = [
        remote(part.at[2, pl.ds(0, TOP)], first.at[0], first_send.at[0], first_recv.at[0], right),
        remote(part.at[2, pl.ds(TOP, TOP)], first.at[1], first_send.at[1], first_recv.at[1], left),
    ]
    for copy in first_copies:
        copy.start()
    for copy in sum_copies:
        copy.start()
    part[1] = partial_of(xr).astype(BF16)
    part[3] = partial_of(xl).astype(BF16)

    def second_copies(q):
        rows = pl.ds(q * STEP, STEP)
        return (
            remote(part.at[1, rows], second.at[0, rows], second_send.at[0, q],
                   second_recv.at[0, q], right),
            remote(part.at[3, rows], second.at[1, rows], second_send.at[1, q],
                   second_recv.at[1, q], left),
        )

    half = PARTS // 2
    for q in range(half):
        second_copies(half + q)[0].start()
        second_copies(q)[1].start()
    arrived(first.at[0], first_recv.at[0])
    arrived(first.at[1], first_recv.at[1])
    for q in range(half):
        rows = pl.ds(q * STEP, STEP)
        low = pl.ds(TOP + q * STEP, STEP)
        part[1, rows] = (part[1, rows].astype(F32) + first[0, rows].astype(F32)).astype(BF16)
        second_copies(q)[0].start()
        part[3, low] = (part[3, low].astype(F32) + first[1, rows].astype(F32)).astype(BF16)
        second_copies(half + q)[1].start()
    own_part[...] = partial_of(x)

    loads[4].wait()
    blank = jnp.zeros((CAND, COLS), BF16)
    wide_rows[0:CAND, 0:COLS] = rows_v[...]
    wide_rows[0:CAND, COLS:2 * COLS] = blank
    wide_rows[CAND:2 * CAND, 0:COLS] = blank
    wide_rows[CAND:2 * CAND, COLS:2 * COLS] = rows_v[...]
    for v in (xl, xr, xo):
        arrived(lab_sum.at[v], sum_recv.at[v])
    rest = jnp.zeros((ROWS, 2 * CAND), F32)
    for v in range(NX):
        rest += lab_sum[v].astype(F32)
    terms = []
    for _ in range(3):
        term = rest.astype(BF16)
        terms.append(term)
        rest = rest - term.astype(F32)
    spread = wide_rows[...]
    corr[...] = (
        jnp.dot(terms[2], spread, preferred_element_type=F32)
        + jnp.dot(terms[1], spread, preferred_element_type=F32)
    ) + jnp.dot(terms[0], spread, preferred_element_type=F32)

    for n in (5, 6, 7, 8):
        loads[n].wait()
    factor = 1.0 / math.sqrt(TOK * NX * NL)

    def out_copy(q, index, n, to):
        piece = wout.at[index, pl.ds(q * STEP, STEP)]
        return remote(piece, piece, out_send.at[q, n], out_recv.at[q, index], to)

    def own_sends(q):
        return [out_copy(q, dp, n, to) for n, to in enumerate(line_dev + [right, left])]

    def line_sends(q):
        return [
            out_copy(q, v * NX + x, 5 + 2 * m + d, to)
            for m, v in enumerate(line) for d, to in enumerate((right, left))
        ]

    def forwards(q):
        order = [zl] + line
        return [
            out_copy(q, v * NX + (xl if m < 2 else xr), 11 + m, right if m < 2 else left)
            for m, v in enumerate(order)
        ]

    def out_arrived(q, index):
        arrived(wout.at[index, pl.ds(q * STEP, STEP)], out_recv.at[q, index])

    def finish(q, carry):
        rows = pl.ds(pl.multiple_of(q * STEP, STEP), STEP)
        arrived(second.at[0, rows], second_recv.at[0, q])
        arrived(second.at[1, rows], second_recv.at[1, q])
        common = (
            own_part[rows, :] + second[0, rows, :].astype(F32) + second[1, rows, :].astype(F32)
        )
        grad_true = (common - corr[rows, 0:COLS]) * factor
        grad_sampled = (common - corr[rows, COLS:2 * COLS]) * factor
        drawn = bits_v[rows, :]
        low = jnp.bitwise_and(drawn, 127)
        high = jnp.right_shift(drawn, 7)
        mixed = jnp.bitwise_and(3 * low + 5 * high, 127)

        def dither(value, noise):
            scale = (noise.astype(F32) + 960.5) * (1.0 / 1024.0)
            return (value * scale).astype(BF16)

        new_moment = dither(
            beta_one * moment_v[rows, :].astype(F32) + (1.0 - beta_one) * grad_true, low
        )
        new_curv = dither(
            beta_two * curv_v[rows, :].astype(F32)
            + (1.0 - beta_two) * grad_sampled * grad_sampled,
            high,
        )
        ratio = jnp.clip(
            new_moment.astype(F32) / (gamma_rate * new_curv.astype(F32)), -1.0, 1.0
        )
        shrunk = (
            weight_v[rows, :].astype(F32) * (1.0 - learn_rate * decay_rate) - learn_rate * ratio
        )
        mout[rows, :] = new_moment
        cout[rows, :] = new_curv
        wout[dp, rows, :] = dither(shrunk, mixed)
        for copy in own_sends(q):
            copy.start()
        return carry

    lax.fori_loop(0, PARTS, finish, 0)

    def pass_line(q):
        for m, v in enumerate(line):
            out_arrived(q, v * NX + x)
            line_sends(q)[2 * m].start()
            line_sends(q)[2 * m + 1].start()

    def pass_ring(q):
        copies = forwards(q)
        for m, v in enumerate([zl] + line):
            out_arrived(q, v * NX + xl)
            out_arrived(q, v * NX + xr)
            copies[m].start()

    def spread_step(t, carry):
        @pl.when(t < PARTS)
        def _():
            pass_line(t)

        @pl.when(t > 0)
        def _():
            pass_ring(t - 1)

        return carry

    lax.fori_loop(0, PARTS + 1, spread_step, 0)

    def last_step(q, carry):
        for v in [zl] + line:
            out_arrived(q, v * NX + xo)
        for copy in own_sends(q) + line_sends(q) + forwards(q):
            copy.wait_send()
        for copy in second_copies(q):
            copy.wait_send()
        return carry

    lax.fori_loop(0, PARTS, last_step, 0)

    for h in range(NH):
        @pl.when(jnp.logical_or(zl != row, zh != h))
        def _():
            for n in range(SUB):
                own_copy(0, h, n).wait_send()

        for n in range(SUB):
            own_copy(1, h, n).wait_send()
    for copy in hid_copies + labs_copies:
        copy.wait_send()
    for copy in sum_copies:
        copy.wait_send()
    for copy in first_copies:
        copy.wait_send()

    def drain_chain(k, carry):
        for yb in (0, 1):
            up_copy, down_copy, sib_copy = chain_copies(yb, k)

            @pl.when(goes_up[yb])
            def _():
                up_copy.wait_send()

            @pl.when(goes_down[yb])
            def _():
                down_copy.wait_send()

            sib_copy.wait_send()

        return carry

    lax.fori_loop(0, BLOCKS, drain_chain, 0)


def place_kernel(wide, moment, curv, wide_out, moment_out, curv_out, sem):
    copies = [
        pltpu.make_async_copy(
            wide.at[n], wide_out.at[:, pl.ds(n * COLS, COLS)], sem.at[n]
        )
        for n in range(NX * NL)
    ]
    copies.append(pltpu.make_async_copy(moment, moment_out, sem.at[NX * NL]))
    copies.append(pltpu.make_async_copy(curv, curv_out, sem.at[NX * NL + 1]))
    for copy in copies:
        copy.start()
    for copy in copies:
        copy.wait()


def on_device(
    gate_up, cot_mean, label_rows, true_labels, sampled_labels, weight, moment, curvature, bits
):
    dma = pltpu.SemaphoreType.DMA
    groups = NX * NL
    anywhere = pl.BlockSpec(memory_space=pl.ANY)
    in_hbm = pl.BlockSpec(memory_space=pltpu.HBM)
    in_vmem = pl.BlockSpec(memory_space=pltpu.VMEM)
    state = (ROWS, COLS)
    pieces, new_moment, new_curv = pl.pallas_call(
        step_kernel,
        out_shape=[
            pltpu.VMEM((groups, ROWS, COLS), BF16),
            pltpu.VMEM(state, BF16),
            pltpu.VMEM(state, BF16),
        ],
        in_specs=[in_hbm] * 9,
        out_specs=[in_vmem] * 3,
        scratch_shapes=[
            pltpu.VMEM((2, ROWS, TOK), BF16),
            pltpu.VMEM((TOK, HALF), BF16),
            pltpu.VMEM((CAND, COLS), BF16),
            pltpu.VMEM((1, TOK), I32),
            pltpu.VMEM((1, TOK), I32),
            pltpu.VMEM(state, BF16),
            pltpu.VMEM(state, BF16),
            pltpu.VMEM(state, BF16),
            pltpu.VMEM(state, I32),
            pltpu.VMEM((NL, ROWS, TOK), BF16),
            pltpu.VMEM((NL, 8, TOK), I32),
            pltpu.VMEM((NX, NC, NL, TOK, HALF), BF16),
            pltpu.VMEM((NX, ROWS, COLS), BF16),
            pltpu.VMEM(state, F32),
            pltpu.VMEM((2, TOP, COLS), BF16),
            pltpu.VMEM((2, ROWS, COLS), BF16),
            pltpu.VMEM((NX, ROWS, 2 * CAND), BF16),
            pltpu.VMEM((2 * CAND, 2 * COLS), BF16),
            pltpu.VMEM((ROWS, 2 * COLS), F32),
            dma((9,)),
            dma((2, NH, SUB)),
            dma((2, NZ, SUB)),
            dma((2, BLOCKS, 2)),
            dma((2, BLOCKS)),
            dma((2, BLOCKS)),
            dma((NL - 1,)),
            dma((NL,)),
            dma((NL - 1,)),
            dma((NL,)),
            dma((3,)),
            dma((NX,)),
            dma((2,)),
            dma((2,)),
            dma((2, PARTS)),
            dma((2, PARTS)),
            dma((PARTS, 15)),
            dma((PARTS, groups)),
        ],
        compiler_params=pltpu.CompilerParams(
            collective_id=0, has_side_effects=True, vmem_limit_bytes=58 * 1024 * 1024
        ),
        cost_estimate=pl.CostEstimate(
            flops=1_000_000_000, bytes_accessed=6_000_000, transcendentals=114_688
        ),
        name="sophia_step",
    )(
        jnp.swapaxes(gate_up, 1, 2), cot_mean, label_rows,
        true_labels.reshape(1, TOK), sampled_labels.reshape(1, TOK),
        weight, moment, curvature, bits,
    )
    return pl.pallas_call(
        place_kernel,
        out_shape=[
            jax.ShapeDtypeStruct((ROWS, groups * COLS), BF16),
            jax.ShapeDtypeStruct(state, BF16),
            jax.ShapeDtypeStruct(state, BF16),
        ],
        in_specs=[anywhere] * 3,
        out_specs=[in_hbm] * 3,
        scratch_shapes=[dma((groups + 2,))],
        compiler_params=pltpu.CompilerParams(vmem_limit_bytes=1024 * 1024),
        name="place",
    )(pieces, new_moment, new_curv)


def solution(mesh):
    in_specs = (
        P(None, "dp", "zero"),
        P("dp", "zero"),
        P(None, "dp"),
        P("dp"),
        P("dp"),
        P("zero", "dp"),
        P("zero", "dp"),
        P("zero", "dp"),
        P("zero", "dp"),
    )
    out_specs = (P("zero", None), P("zero", "dp"), P("zero", "dp"))
    return jax.shard_map(
        on_device, mesh=mesh, in_specs=in_specs, out_specs=out_specs, check_vma=False
    )
```

```python
import math

import jax
import jax.numpy as jnp
from jax import lax
from jax.experimental import pallas as pl
from jax.experimental.pallas import tpu as pltpu
from jax.sharding import PartitionSpec as P

beta_one = 0.965
beta_two = 0.99
gamma_rate = 0.5
learn_rate = 0.05
decay_rate = 0.1

NX, NL, NY, NH, NC = 4, 4, 8, 2, 2
NZ = NH * NL
ROWS, TOK, COLS, HALF, CAND = 448, 256, 256, 128, 64
PARTS = 4
SUB, LAG = 1, 3
HID_AT, CUT_AT = 4, 11
BLOCKS = NZ * SUB
FINE = TOK // SUB
STEP = ROWS // PARTS
TOP = ROWS // 2
BF16, F32, I32 = jnp.bfloat16, jnp.float32, jnp.int32


def device(x, y, zh, zl, core):
    return (zl * NX + x, (y * NH + zh) * NC + core)


def remote(src, dst, send, recv, to):
    return pltpu.make_async_remote_copy(
        src, dst, send, recv, device_id=to, device_id_type=pl.DeviceIdType.MESH
    )


def arrived(dst, sem):
    pltpu.make_async_copy(dst, dst, sem).wait()


def step_kernel(
    gate_in, cot_in, rows_in, true_in, sampled_in, weight_in, moment_in, curv_in, bits_in,
    wout, mout, cout,
    gate_v, cot_v, rows_v, true_v, sampled_v, weight_v, moment_v, curv_v, bits_v,
    hid, cot, part, own_part, first, second, lab_own, lab_cut, lab_sum, lab_all,
    wide_rows, corr,
    load_sem, own_cot_send, cot_recv, chain_send, sib_send, sib_recv,
    hid_send, hid_recv, cut_send, cut_recv, sum_send, sum_recv, all_send, all_recv,
    first_send, first_recv, second_send, second_recv, out_send, out_recv,
):
    dp = lax.axis_index("dp")
    zero = lax.axis_index("zero")
    x, zl = dp % NX, dp // NX
    core, zh, y = zero % NC, (zero // NC) % NH, zero // (NC * NH)
    z = zh * NL + zl
    xr, xo, xl = (x + 1) % NX, (x + 2) % NX, (x + 3) % NX
    right, across, left = [device(v, y, zh, zl, core) for v in (xr, xo, xl)]
    y_up, y_down = [device(x, (y + d) % NY, zh, zl, core) for d in (1, NY - 1)]
    sibling = device(x, y, zh, zl, 1 - core)
    line = [zl + 1 - 2 * (zl % 2), (zl + 2) % NL, NL - 1 - zl]
    line_dev = [device(x, y, zh, v, core) for v in line]

    loads = [
        pltpu.make_async_copy(src, dst, load_sem.at[n])
        for n, (src, dst) in enumerate([
            (cot_in, cot_v), (gate_in, gate_v), (true_in, true_v), (sampled_in, sampled_v),
            (rows_in, rows_v), (moment_in, moment_v), (curv_in, curv_v), (bits_in, bits_v),
            (weight_in, weight_v),
        ])
    ]
    for load in loads:
        load.start()

    barrier = pltpu.get_barrier_semaphore()
    y_far = (y + NY // 2) % NY
    row = y // 2

    def greet(partner):
        pl.semaphore_signal(
            barrier, inc=1, device_id=partner, device_id_type=pl.DeviceIdType.MESH
        )

    for y_from, at_row in ((y_far, zl == y_far // 2), (y, zl == row)):
        @pl.when(at_row)
        def _():
            for k in (4, 3, 5, 2, 6, 1, 7):
                other = (z + k) % NZ
                greet(device(x, y_from, other // NL, other % NL, core))

    @pl.when(zl == y_far // 2)
    def _():
        greet(device(x, y_far, zh, zl, core))

    partners = [right, across, left, y_up, y_down, sibling] + line_dev
    for partner in partners:
        greet(partner)
    greeted = len(partners) + 2 * NH - (zl == row).astype(I32)

    loads[1].wait()
    gate = gate_v[0].astype(F32)
    up = gate_v[1].astype(F32)
    hid[zl] = (jax.nn.silu(gate) * up).astype(BF16)
    hid_copies = [
        remote(hid.at[zl], hid.at[zl], hid_send.at[k], hid_recv.at[zl], line_dev[k])
        for k in range(NL - 1)
    ]
    loads[2].wait()
    loads[3].wait()
    classes = lax.broadcasted_iota(I32, (CAND, TOK), 0)
    hot = jnp.concatenate(
        [(classes == lab[...]).astype(F32) for lab in (true_v, sampled_v)], axis=0
    ).astype(BF16)
    label_part = lax.dot_general(
        hid[zl], hot, (((1,), (1,)), ((), ())), preferred_element_type=F32
    )
    for v in range(NL):
        lab_own[v] = label_part[v * STEP:(v + 1) * STEP].astype(BF16)
    cut_copies = [
        remote(lab_own.at[v], lab_cut.at[zl], cut_send.at[k], cut_recv.at[zl], line_dev[k])
        for k, v in enumerate(line)
    ]
    lab_cut[zl] = lab_own[zl]
    ring = [xr, xo, xl]
    sum_copies = [
        remote(lab_sum.at[x], lab_sum.at[x], sum_send.at[k], sum_recv.at[x], to)
        for k, to in enumerate((right, across, left))
    ]
    all_copies = [
        remote(lab_all.at[zl], lab_all.at[zl], all_send.at[k], all_recv.at[zl], to)
        for k, to in enumerate(line_dev)
    ]

    loads[0].wait()
    pl.semaphore_wait(barrier, greeted)

    own_slot = cot.at[(y % 2) * 2 + zh, core, zl]

    def fine_of(ref, n):
        return ref.at[pl.ds(n * FINE, FINE)]

    def own_copy(far, h, n):
        return remote(
            fine_of(cot_v, n), fine_of(own_slot, n), own_cot_send.at[far, h, n],
            cot_recv.at[y % 2, z, n], device(x, (y, y_far)[far], h, row, core),
        )

    for h in range(NH):
        @pl.when(jnp.logical_or(zl != row, zh != h))
        def _():
            for n in range(SUB):
                own_copy(0, h, n).start()

        for n in range(SUB):
            own_copy(1, h, n).start()

    @pl.when(zl == row)
    def _():
        for n in range(SUB):
            pltpu.make_async_copy(
                fine_of(cot_v, n), fine_of(own_slot, n), cot_recv.at[y % 2, z, n]
            ).start()

    for copy in cut_copies:
        copy.start()

    place = (y - 2 * zl + NY) % (NY // 2)
    lag = (
        jnp.where(place == 1, 1, (4 - place) % 4),
        jnp.where(place == 0, 1, place - 1),
    )
    goes_up = (place == 0, jnp.logical_or(place == 1, place == 2))
    goes_down = (jnp.logical_or(place == 0, place == 3), place == 1)

    def slot_of(yb, k, half):
        step, n = k // SUB, k % SUB
        src = jnp.where(step % 2 == 1, z + (step + 1) // 2, z + NZ - step // 2) % NZ
        return cot.at[yb * 2 + src // NL, half, src % NL, pl.ds(n * FINE, FINE)], src, n

    def chain_copies(yb, k):
        slot, src, n = slot_of(yb, k, core)
        return (
            remote(slot, slot, chain_send.at[yb, k, 0], cot_recv.at[yb, src, n], y_up),
            remote(slot, slot, chain_send.at[yb, k, 1], cot_recv.at[yb, src, n], y_down),
            remote(slot, slot, sib_send.at[yb, k], sib_recv.at[yb, k], sibling),
        )

    def chain_step(t, carry):
        for yb in (0, 1):
            k = t - LAG * lag[yb]

            @pl.when(jnp.logical_and(k >= 0, k < BLOCKS))
            def _():
                slot, src, n = slot_of(yb, k, core)
                arrived(slot, cot_recv.at[yb, src, n])
                up_copy, down_copy, sib_copy = chain_copies(yb, k)

                @pl.when(goes_up[yb])
                def _():
                    up_copy.start()

                @pl.when(goes_down[yb])
                def _():
                    down_copy.start()

                sib_copy.start()

        return carry

    lax.fori_loop(0, HID_AT, chain_step, 0)
    for copy in hid_copies:
        copy.start()
    lax.fori_loop(HID_AT, CUT_AT, chain_step, 0)
    for v in line:
        arrived(lab_cut.at[v], cut_recv.at[v])
    quarter = lab_cut[0].astype(F32)
    for v in range(1, NL):
        quarter += lab_cut[v].astype(F32)
    lab_sum[x] = quarter
    for copy in sum_copies:
        copy.start()
    lax.fori_loop(CUT_AT, BLOCKS + 2 * LAG, chain_step, 0)

    for v in line:
        arrived(hid.at[v], hid_recv.at[v])

    def wait_sibling(k, carry):
        for yb in (0, 1):
            arrived(slot_of(yb, k, 1 - core)[0], sib_recv.at[yb, k])
        return carry

    lax.fori_loop(0, BLOCKS, wait_sibling, 0)

    def partial_of(owner):
        acc = jnp.zeros((ROWS, COLS), F32)
        for v in range(NL):
            wide = jnp.concatenate([cot[owner, 0, v], cot[owner, 1, v]], axis=1)
            acc += jnp.dot(hid[v], wide, preferred_element_type=F32)
        return acc

    part[2] = partial_of(xo).astype(BF16)
    first_copies = [
        remote(part.at[2, pl.ds(0, TOP)], first.at[0], first_send.at[0], first_recv.at[0], right),
        remote(part.at[2, pl.ds(TOP, TOP)], first.at[1], first_send.at[1], first_recv.at[1], left),
    ]
    for copy in first_copies:
        copy.start()
    part[1] = partial_of(xr).astype(BF16)
    part[3] = partial_of(xl).astype(BF16)

    def second_copies(q):
        rows = pl.ds(q * STEP, STEP)
        return (
            remote(part.at[1, rows], second.at[0, rows], second_send.at[0, q],
                   second_recv.at[0, q], right),
            remote(part.at[3, rows], second.at[1, rows], second_send.at[1, q],
                   second_recv.at[1, q], left),
        )

    half = PARTS // 2
    for q in range(half):
        second_copies(half + q)[0].start()
        second_copies(q)[1].start()
    for v in ring:
        arrived(lab_sum.at[v], sum_recv.at[v])
    lab_all[zl] = (lab_sum[0] + lab_sum[1]) + (lab_sum[2] + lab_sum[3])
    for copy in all_copies:
        copy.start()
    arrived(first.at[0], first_recv.at[0])
    arrived(first.at[1], first_recv.at[1])
    for q in range(half):
        rows = pl.ds(q * STEP, STEP)
        low = pl.ds(TOP + q * STEP, STEP)
        part[1, rows] = (part[1, rows].astype(F32) + first[0, rows].astype(F32)).astype(BF16)
        second_copies(q)[0].start()
        part[3, low] = (part[3, low].astype(F32) + first[1, rows].astype(F32)).astype(BF16)
        second_copies(half + q)[1].start()
    own_part[...] = partial_of(x)

    loads[4].wait()
    blank = jnp.zeros((CAND, COLS), BF16)
    wide_rows[0:CAND, 0:COLS] = rows_v[...]
    wide_rows[0:CAND, COLS:2 * COLS] = blank
    wide_rows[CAND:2 * CAND, 0:COLS] = blank
    wide_rows[CAND:2 * CAND, COLS:2 * COLS] = rows_v[...]
    for v in line:
        arrived(lab_all.at[v], all_recv.at[v])
    rest = lab_all[...].reshape(ROWS, 2 * CAND)
    terms = []
    for _ in range(3):
        term = rest.astype(BF16)
        terms.append(term)
        rest = rest - term.astype(F32)
    spread = wide_rows[...]
    corr[...] = (
        jnp.dot(terms[2], spread, preferred_element_type=F32)
        + jnp.dot(terms[1], spread, preferred_element_type=F32)
    ) + jnp.dot(terms[0], spread, preferred_element_type=F32)

    for n in (5, 6, 7, 8):
        loads[n].wait()
    factor = 1.0 / math.sqrt(TOK * NX * NL)

    def out_copy(q, index, n, to):
        piece = wout.at[index, pl.ds(q * STEP, STEP)]
        return remote(piece, piece, out_send.at[q, n], out_recv.at[q, index], to)

    def own_sends(q):
        return [out_copy(q, dp, n, to) for n, to in enumerate(line_dev + [right, left])]

    def line_sends(q):
        return [
            out_copy(q, v * NX + x, 5 + 2 * m + d, to)
            for m, v in enumerate(line) for d, to in enumerate((right, left))
        ]

    def forwards(q):
        swap = q % 2 == 1
        copies = []
        for m, v in enumerate([zl] + line):
            copies.append((
                jnp.logical_xor(swap, m < 2),
                out_copy(q, v * NX + xl, 11 + m, right),
                out_copy(q, v * NX + xr, 11 + m, left),
            ))
        return copies

    def out_arrived(q, index):
        arrived(wout.at[index, pl.ds(q * STEP, STEP)], out_recv.at[q, index])

    def finish(q, carry):
        rows = pl.ds(pl.multiple_of(q * STEP, STEP), STEP)
        arrived(second.at[0, rows], second_recv.at[0, q])
        arrived(second.at[1, rows], second_recv.at[1, q])
        common = (
            own_part[rows, :] + second[0, rows, :].astype(F32) + second[1, rows, :].astype(F32)
        )
        grad_true = (common - corr[rows, 0:COLS]) * factor
        grad_sampled = (common - corr[rows, COLS:2 * COLS]) * factor
        drawn = bits_v[rows, :]
        low = jnp.bitwise_and(drawn, 127)
        high = jnp.right_shift(drawn, 7)
        mixed = jnp.bitwise_and(3 * low + 5 * high, 127)

        def dither(value, noise):
            scale = (noise.astype(F32) + 960.5) * (1.0 / 1024.0)
            return (value * scale).astype(BF16)

        new_moment = dither(
            beta_one * moment_v[rows, :].astype(F32) + (1.0 - beta_one) * grad_true, low
        )
        new_curv = dither(
            beta_two * curv_v[rows, :].astype(F32)
            + (1.0 - beta_two) * grad_sampled * grad_sampled,
            high,
        )
        ratio = jnp.clip(
            new_moment.astype(F32) / (gamma_rate * new_curv.astype(F32)), -1.0, 1.0
        )
        shrunk = (
            weight_v[rows, :].astype(F32) * (1.0 - learn_rate * decay_rate) - learn_rate * ratio
        )
        mout[rows, :] = new_moment
        cout[rows, :] = new_curv
        wout[dp, rows, :] = dither(shrunk, mixed)
        for copy in own_sends(q):
            copy.start()
        return carry

    lax.fori_loop(0, PARTS, finish, 0)

    def pass_line(q):
        for m, v in enumerate(line):
            out_arrived(q, v * NX + x)
            line_sends(q)[2 * m].start()
            line_sends(q)[2 * m + 1].start()

    def pass_ring(q):
        for (rightward, to_right, to_left), v in zip(forwards(q), [zl] + line):
            @pl.when(rightward)
            def _():
                out_arrived(q, v * NX + xl)
                to_right.start()

            @pl.when(jnp.logical_not(rightward))
            def _():
                out_arrived(q, v * NX + xr)
                to_left.start()

    def spread_step(t, carry):
        @pl.when(t < PARTS)
        def _():
            pass_line(t)

        @pl.when(t > 0)
        def _():
            pass_ring(t - 1)

        return carry

    lax.fori_loop(0, PARTS + 1, spread_step, 0)

    def last_step(q, carry):
        for (rightward, to_right, to_left), v in zip(forwards(q), [zl] + line):
            out_arrived(q, v * NX + jnp.where(rightward, xr, xl))
            out_arrived(q, v * NX + xo)
            to_right.wait_send()
        for copy in own_sends(q) + line_sends(q):
            copy.wait_send()
        for copy in second_copies(q):
            copy.wait_send()
        return carry

    lax.fori_loop(0, PARTS, last_step, 0)

    for h in range(NH):
        @pl.when(jnp.logical_or(zl != row, zh != h))
        def _():
            for n in range(SUB):
                own_copy(0, h, n).wait_send()

        for n in range(SUB):
            own_copy(1, h, n).wait_send()
    for copy in hid_copies:
        copy.wait_send()
    for copy in cut_copies + sum_copies + all_copies:
        copy.wait_send()
    for copy in first_copies:
        copy.wait_send()

    def drain_chain(k, carry):
        for yb in (0, 1):
            up_copy, down_copy, sib_copy = chain_copies(yb, k)

            @pl.when(goes_up[yb])
            def _():
                up_copy.wait_send()

            @pl.when(goes_down[yb])
            def _():
                down_copy.wait_send()

            sib_copy.wait_send()

        return carry

    lax.fori_loop(0, BLOCKS, drain_chain, 0)


def place_kernel(wide, moment, curv, wide_out, moment_out, curv_out, sem):
    copies = [
        pltpu.make_async_copy(
            wide.at[n], wide_out.at[:, pl.ds(n * COLS, COLS)], sem.at[n]
        )
        for n in range(NX * NL)
    ]
    copies.append(pltpu.make_async_copy(moment, moment_out, sem.at[NX * NL]))
    copies.append(pltpu.make_async_copy(curv, curv_out, sem.at[NX * NL + 1]))
    for copy in copies:
        copy.start()
    for copy in copies:
        copy.wait()


def on_device(
    gate_up, cot_mean, label_rows, true_labels, sampled_labels, weight, moment, curvature, bits
):
    dma = pltpu.SemaphoreType.DMA
    groups = NX * NL
    anywhere = pl.BlockSpec(memory_space=pl.ANY)
    in_hbm = pl.BlockSpec(memory_space=pltpu.HBM)
    in_vmem = pl.BlockSpec(memory_space=pltpu.VMEM)
    state = (ROWS, COLS)
    pieces, new_moment, new_curv = pl.pallas_call(
        step_kernel,
        out_shape=[
            pltpu.VMEM((groups, ROWS, COLS), BF16),
            pltpu.VMEM(state, BF16),
            pltpu.VMEM(state, BF16),
        ],
        in_specs=[in_hbm] * 9,
        out_specs=[in_vmem] * 3,
        scratch_shapes=[
            pltpu.VMEM((2, ROWS, TOK), BF16),
            pltpu.VMEM((TOK, HALF), BF16),
            pltpu.VMEM((CAND, COLS), BF16),
            pltpu.VMEM((1, TOK), I32),
            pltpu.VMEM((1, TOK), I32),
            pltpu.VMEM(state, BF16),
            pltpu.VMEM(state, BF16),
            pltpu.VMEM(state, BF16),
            pltpu.VMEM(state, I32),
            pltpu.VMEM((NL, ROWS, TOK), BF16),
            pltpu.VMEM((NX, NC, NL, TOK, HALF), BF16),
            pltpu.VMEM((NX, ROWS, COLS), BF16),
            pltpu.VMEM(state, F32),
            pltpu.VMEM((2, TOP, COLS), BF16),
            pltpu.VMEM((2, ROWS, COLS), BF16),
            pltpu.VMEM((NL, STEP, 2 * CAND), BF16),
            pltpu.VMEM((NL, STEP, 2 * CAND), BF16),
            pltpu.VMEM((NX, STEP, 2 * CAND), F32),
            pltpu.VMEM((NL, STEP, 2 * CAND), F32),
            pltpu.VMEM((2 * CAND, 2 * COLS), BF16),
            pltpu.VMEM((ROWS, 2 * COLS), F32),
            dma((9,)),
            dma((2, NH, SUB)),
            dma((2, NZ, SUB)),
            dma((2, BLOCKS, 2)),
            dma((2, BLOCKS)),
            dma((2, BLOCKS)),
            dma((NL - 1,)),
            dma((NL,)),
            dma((NL - 1,)),
            dma((NL,)),
            dma((NX - 1,)),
            dma((NX,)),
            dma((NL - 1,)),
            dma((NL,)),
            dma((2,)),
            dma((2,)),
            dma((2, PARTS)),
            dma((2, PARTS)),
            dma((PARTS, 15)),
            dma((PARTS, groups)),
        ],
        compiler_params=pltpu.CompilerParams(
            collective_id=0, has_side_effects=True, vmem_limit_bytes=58 * 1024 * 1024
        ),
        cost_estimate=pl.CostEstimate(
            flops=1_000_000_000, bytes_accessed=6_000_000, transcendentals=114_688
        ),
        name="sophia_step",
    )(
        jnp.swapaxes(gate_up, 1, 2), cot_mean, label_rows,
        true_labels.reshape(1, TOK), sampled_labels.reshape(1, TOK),
        weight, moment, curvature, bits,
    )
    return pl.pallas_call(
        place_kernel,
        out_shape=[
            jax.ShapeDtypeStruct((ROWS, groups * COLS), BF16),
            jax.ShapeDtypeStruct(state, BF16),
            jax.ShapeDtypeStruct(state, BF16),
        ],
        in_specs=[anywhere] * 3,
        out_specs=[in_hbm] * 3,
        scratch_shapes=[dma((groups + 2,))],
        compiler_params=pltpu.CompilerParams(vmem_limit_bytes=1024 * 1024),
        name="place",
    )(pieces, new_moment, new_curv)


def solution(mesh):
    in_specs = (
        P(None, "dp", "zero"),
        P("dp", "zero"),
        P(None, "dp"),
        P("dp"),
        P("dp"),
        P("zero", "dp"),
        P("zero", "dp"),
        P("zero", "dp"),
        P("zero", "dp"),
    )
    out_specs = (P("zero", None), P("zero", "dp"), P("zero", "dp"))
    return jax.shard_map(
        on_device, mesh=mesh, in_specs=in_specs, out_specs=out_specs, check_vma=False
    )
```

```python
import math

import jax
import jax.numpy as jnp
from jax import lax
from jax.experimental import pallas as pl
from jax.experimental.pallas import tpu as pltpu
from jax.sharding import PartitionSpec as P

beta_one = 0.965
beta_two = 0.99
gamma_rate = 0.5
learn_rate = 0.05
decay_rate = 0.1

NX, NL, NY, NH, NC = 4, 4, 8, 2, 2
NZ = NH * NL
ROWS, TOK, COLS, HALF, CAND = 448, 256, 256, 128, 64
PARTS = 4
SUB, LAG = 1, 3
HID_AT, CUT_AT = 5, 14
BLOCKS = NZ * SUB
FINE = TOK // SUB
STEP = ROWS // PARTS
TOP = ROWS // 2
BF16, F32, I32 = jnp.bfloat16, jnp.float32, jnp.int32


def device(x, y, zh, zl, core):
    return (zl * NX + x, (y * NH + zh) * NC + core)


def remote(src, dst, send, recv, to):
    return pltpu.make_async_remote_copy(
        src, dst, send, recv, device_id=to, device_id_type=pl.DeviceIdType.MESH
    )


def arrived(dst, sem):
    pltpu.make_async_copy(dst, dst, sem).wait()


def step_kernel(
    gate_in, cot_in, rows_in, true_in, sampled_in, weight_in, moment_in, curv_in, bits_in,
    wout, mout, cout,
    gate_v, cot_v, rows_v, true_v, sampled_v, weight_v, moment_v, curv_v, bits_v,
    hid, cot, part, own_part, first, second, lab_own, lab_cut, lab_sum, lab_all,
    wide_rows, corr,
    load_sem, own_cot_send, cot_recv, chain_send, sib_send, sib_recv,
    hid_send, hid_recv, cut_send, cut_recv, sum_send, sum_recv, all_send, all_recv,
    first_send, first_recv, second_send, second_recv, out_send, out_recv,
):
    dp = lax.axis_index("dp")
    zero = lax.axis_index("zero")
    x, zl = dp % NX, dp // NX
    core, zh, y = zero % NC, (zero // NC) % NH, zero // (NC * NH)
    z = zh * NL + zl
    xr, xo, xl = (x + 1) % NX, (x + 2) % NX, (x + 3) % NX
    right, across, left = [device(v, y, zh, zl, core) for v in (xr, xo, xl)]
    y_up, y_down = [device(x, (y + d) % NY, zh, zl, core) for d in (1, NY - 1)]
    sibling = device(x, y, zh, zl, 1 - core)
    line = [zl + 1 - 2 * (zl % 2), (zl + 2) % NL, NL - 1 - zl]
    line_dev = [device(x, y, zh, v, core) for v in line]

    loads = [
        pltpu.make_async_copy(src, dst, load_sem.at[n])
        for n, (src, dst) in enumerate([
            (cot_in, cot_v), (gate_in, gate_v), (true_in, true_v), (sampled_in, sampled_v),
            (rows_in, rows_v), (moment_in, moment_v), (curv_in, curv_v), (bits_in, bits_v),
            (weight_in, weight_v),
        ])
    ]
    for load in loads:
        load.start()

    barrier = pltpu.get_barrier_semaphore()
    y_far = (y + NY // 2) % NY
    row = y // 2

    def greet(partner):
        pl.semaphore_signal(
            barrier, inc=1, device_id=partner, device_id_type=pl.DeviceIdType.MESH
        )

    for y_from, at_row in ((y_far, zl == y_far // 2), (y, zl == row)):
        @pl.when(at_row)
        def _():
            for k in (4, 3, 5, 2, 6, 1, 7):
                other = (z + k) % NZ
                greet(device(x, y_from, other // NL, other % NL, core))

    @pl.when(zl == y_far // 2)
    def _():
        greet(device(x, y_far, zh, zl, core))

    partners = [right, across, left, y_up, y_down, sibling] + line_dev
    for partner in partners:
        greet(partner)
    greeted = len(partners) + 2 * NH - (zl == row).astype(I32)

    loads[1].wait()
    gate = gate_v[0].astype(F32)
    up = gate_v[1].astype(F32)
    hid[zl] = (jax.nn.silu(gate) * up).astype(BF16)
    hid_copies = [
        remote(hid.at[zl], hid.at[zl], hid_send.at[k], hid_recv.at[zl], line_dev[k])
        for k in range(NL - 1)
    ]
    loads[2].wait()
    loads[3].wait()
    classes = lax.broadcasted_iota(I32, (CAND, TOK), 0)
    hot = jnp.concatenate(
        [(classes == lab[...]).astype(F32) for lab in (true_v, sampled_v)], axis=0
    ).astype(BF16)
    label_part = lax.dot_general(
        hid[zl], hot, (((1,), (1,)), ((), ())), preferred_element_type=F32
    )
    for v in range(NL):
        lab_own[v] = label_part[v * STEP:(v + 1) * STEP].astype(BF16)
    cut_copies = [
        remote(lab_own.at[v], lab_cut.at[zl], cut_send.at[k], cut_recv.at[zl], line_dev[k])
        for k, v in enumerate(line)
    ]
    lab_cut[zl] = lab_own[zl]
    ring = [xr, xo, xl]
    sum_copies = [
        remote(lab_sum.at[x], lab_sum.at[x], sum_send.at[k], sum_recv.at[x], to)
        for k, to in enumerate((right, across, left))
    ]
    all_copies = [
        remote(lab_all.at[zl], lab_all.at[zl], all_send.at[k], all_recv.at[zl], to)
        for k, to in enumerate(line_dev)
    ]

    loads[0].wait()
    pl.semaphore_wait(barrier, greeted)

    own_slot = cot.at[(y % 2) * 2 + zh, core, zl]

    def fine_of(ref, n):
        return ref.at[pl.ds(n * FINE, FINE)]

    def own_copy(far, h, n):
        return remote(
            fine_of(cot_v, n), fine_of(own_slot, n), own_cot_send.at[far, h, n],
            cot_recv.at[y % 2, z, n], device(x, (y, y_far)[far], h, row, core),
        )

    for h in range(NH):
        @pl.when(jnp.logical_or(zl != row, zh != h))
        def _():
            for n in range(SUB):
                own_copy(0, h, n).start()

        for n in range(SUB):
            own_copy(1, h, n).start()

    @pl.when(zl == row)
    def _():
        for n in range(SUB):
            pltpu.make_async_copy(
                fine_of(cot_v, n), fine_of(own_slot, n), cot_recv.at[y % 2, z, n]
            ).start()

    for copy in cut_copies:
        copy.start()

    place = (y - 2 * zl + NY) % (NY // 2)
    lag = (
        jnp.where(place == 1, 1, (4 - place) % 4),
        jnp.where(place == 0, 1, place - 1),
    )
    goes_up = (place == 0, jnp.logical_or(place == 1, place == 2))
    goes_down = (jnp.logical_or(place == 0, place == 3), place == 1)

    def slot_of(yb, k, half):
        step, n = k // SUB, k % SUB
        src = jnp.where(step % 2 == 1, z + (step + 1) // 2, z + NZ - step // 2) % NZ
        return cot.at[yb * 2 + src // NL, half, src % NL, pl.ds(n * FINE, FINE)], src, n

    def chain_copies(yb, k):
        slot, src, n = slot_of(yb, k, core)
        return (
            remote(slot, slot, chain_send.at[yb, k, 0], cot_recv.at[yb, src, n], y_up),
            remote(slot, slot, chain_send.at[yb, k, 1], cot_recv.at[yb, src, n], y_down),
            remote(slot, slot, sib_send.at[yb, k], sib_recv.at[yb, k], sibling),
        )

    def chain_step(t, carry):
        for yb in (0, 1):
            k = t - LAG * lag[yb]

            @pl.when(jnp.logical_and(k >= 0, k < BLOCKS))
            def _():
                slot, src, n = slot_of(yb, k, core)
                arrived(slot, cot_recv.at[yb, src, n])
                up_copy, down_copy, sib_copy = chain_copies(yb, k)

                @pl.when(goes_up[yb])
                def _():
                    up_copy.start()

                @pl.when(goes_down[yb])
                def _():
                    down_copy.start()

                sib_copy.start()

        return carry

    lax.fori_loop(0, HID_AT, chain_step, 0)
    for copy in hid_copies:
        copy.start()
    lax.fori_loop(HID_AT, CUT_AT, chain_step, 0)
    for v in line:
        arrived(lab_cut.at[v], cut_recv.at[v])
    quarter = lab_cut[0].astype(F32)
    for v in range(1, NL):
        quarter += lab_cut[v].astype(F32)
    lab_sum[x] = quarter
    for copy in sum_copies:
        copy.start()
    lax.fori_loop(CUT_AT, BLOCKS + 2 * LAG, chain_step, 0)

    for v in line:
        arrived(hid.at[v], hid_recv.at[v])

    def wait_sibling(k, carry):
        for yb in (0, 1):
            arrived(slot_of(yb, k, 1 - core)[0], sib_recv.at[yb, k])
        return carry

    lax.fori_loop(0, BLOCKS, wait_sibling, 0)

    def partial_of(owner):
        acc = jnp.zeros((ROWS, COLS), F32)
        for v in range(NL):
            wide = jnp.concatenate([cot[owner, 0, v], cot[owner, 1, v]], axis=1)
            acc += jnp.dot(hid[v], wide, preferred_element_type=F32)
        return acc

    part[2] = partial_of(xo).astype(BF16)
    first_copies = [
        remote(part.at[2, pl.ds(0, TOP)], first.at[0], first_send.at[0], first_recv.at[0], right),
        remote(part.at[2, pl.ds(TOP, TOP)], first.at[1], first_send.at[1], first_recv.at[1], left),
    ]
    for copy in first_copies:
        copy.start()
    part[1] = partial_of(xr).astype(BF16)
    part[3] = partial_of(xl).astype(BF16)

    def second_copies(q):
        rows = pl.ds(q * STEP, STEP)
        return (
            remote(part.at[1, rows], second.at[0, rows], second_send.at[0, q],
                   second_recv.at[0, q], right),
            remote(part.at[3, rows], second.at[1, rows], second_send.at[1, q],
                   second_recv.at[1, q], left),
        )

    half = PARTS // 2
    for q in range(half):
        second_copies(half + q)[0].start()
        second_copies(q)[1].start()
    for v in ring:
        arrived(lab_sum.at[v], sum_recv.at[v])
    lab_all[zl] = (lab_sum[0] + lab_sum[1]) + (lab_sum[2] + lab_sum[3])
    for copy in all_copies:
        copy.start()
    arrived(first.at[0], first_recv.at[0])
    arrived(first.at[1], first_recv.at[1])
    for q in range(half):
        rows = pl.ds(q * STEP, STEP)
        low = pl.ds(TOP + q * STEP, STEP)
        part[1, rows] = (part[1, rows].astype(F32) + first[0, rows].astype(F32)).astype(BF16)
        second_copies(q)[0].start()
        part[3, low] = (part[3, low].astype(F32) + first[1, rows].astype(F32)).astype(BF16)
        second_copies(half + q)[1].start()
    own_part[...] = partial_of(x)

    loads[4].wait()
    blank = jnp.zeros((CAND, COLS), BF16)
    wide_rows[0:CAND, 0:COLS] = rows_v[...]
    wide_rows[0:CAND, COLS:2 * COLS] = blank
    wide_rows[CAND:2 * CAND, 0:COLS] = blank
    wide_rows[CAND:2 * CAND, COLS:2 * COLS] = rows_v[...]
    for v in line:
        arrived(lab_all.at[v], all_recv.at[v])
    rest = lab_all[...].reshape(ROWS, 2 * CAND)
    terms = []
    for _ in range(3):
        term = rest.astype(BF16)
        terms.append(term)
        rest = rest - term.astype(F32)
    spread = wide_rows[...]
    corr[...] = (
        jnp.dot(terms[2], spread, preferred_element_type=F32)
        + jnp.dot(terms[1], spread, preferred_element_type=F32)
    ) + jnp.dot(terms[0], spread, preferred_element_type=F32)

    for n in (5, 6, 7, 8):
        loads[n].wait()
    factor = 1.0 / math.sqrt(TOK * NX * NL)

    def out_copy(q, index, n, to):
        piece = wout.at[index, pl.ds(q * STEP, STEP)]
        return remote(piece, piece, out_send.at[q, n], out_recv.at[q, index], to)

    def own_sends(q):
        return [out_copy(q, dp, n, to) for n, to in enumerate(line_dev + [right, left])]

    def line_sends(q):
        return [
            out_copy(q, v * NX + x, 5 + 2 * m + d, to)
            for m, v in enumerate(line) for d, to in enumerate((right, left))
        ]

    def forwards(q):
        swap = q % 2 == 1
        copies = []
        for m, v in enumerate([zl] + line):
            copies.append((
                jnp.logical_xor(swap, m < 2),
                out_copy(q, v * NX + xl, 11 + m, right),
                out_copy(q, v * NX + xr, 11 + m, left),
            ))
        return copies

    def out_arrived(q, index):
        arrived(wout.at[index, pl.ds(q * STEP, STEP)], out_recv.at[q, index])

    def finish(q, carry):
        rows = pl.ds(pl.multiple_of(q * STEP, STEP), STEP)
        arrived(second.at[0, rows], second_recv.at[0, q])
        arrived(second.at[1, rows], second_recv.at[1, q])
        common = (
            own_part[rows, :] + second[0, rows, :].astype(F32) + second[1, rows, :].astype(F32)
        )
        grad_true = (common - corr[rows, 0:COLS]) * factor
        grad_sampled = (common - corr[rows, COLS:2 * COLS]) * factor
        drawn = bits_v[rows, :]
        low = jnp.bitwise_and(drawn, 127)
        high = jnp.right_shift(drawn, 7)
        mixed = jnp.bitwise_and(3 * low + 5 * high, 127)

        def dither(value, noise):
            scale = (noise.astype(F32) + 960.5) * (1.0 / 1024.0)
            return (value * scale).astype(BF16)

        new_moment = dither(
            beta_one * moment_v[rows, :].astype(F32) + (1.0 - beta_one) * grad_true, low
        )
        new_curv = dither(
            beta_two * curv_v[rows, :].astype(F32)
            + (1.0 - beta_two) * grad_sampled * grad_sampled,
            high,
        )
        ratio = jnp.clip(
            new_moment.astype(F32) / (gamma_rate * new_curv.astype(F32)), -1.0, 1.0
        )
        shrunk = (
            weight_v[rows, :].astype(F32) * (1.0 - learn_rate * decay_rate) - learn_rate * ratio
        )
        mout[rows, :] = new_moment
        cout[rows, :] = new_curv
        wout[dp, rows, :] = dither(shrunk, mixed)
        for copy in own_sends(q):
            copy.start()
        return carry

    lax.fori_loop(0, PARTS, finish, 0)

    def pass_line(q):
        for m, v in enumerate(line):
            out_arrived(q, v * NX + x)
            line_sends(q)[2 * m].start()
            line_sends(q)[2 * m + 1].start()

    def pass_ring(q):
        for (rightward, to_right, to_left), v in zip(forwards(q), [zl] + line):
            @pl.when(rightward)
            def _():
                out_arrived(q, v * NX + xl)
                to_right.start()

            @pl.when(jnp.logical_not(rightward))
            def _():
                out_arrived(q, v * NX + xr)
                to_left.start()

    def spread_step(t, carry):
        @pl.when(t < PARTS)
        def _():
            pass_line(t)

        @pl.when(t > 0)
        def _():
            pass_ring(t - 1)

        return carry

    def second_drain(q, carry):
        for copy in second_copies(q):
            copy.wait_send()
        return carry

    lax.fori_loop(0, PARTS, second_drain, 0)

    for h in range(NH):
        @pl.when(jnp.logical_or(zl != row, zh != h))
        def _():
            for n in range(SUB):
                own_copy(0, h, n).wait_send()

        for n in range(SUB):
            own_copy(1, h, n).wait_send()
    for copy in hid_copies:
        copy.wait_send()
    for copy in cut_copies + sum_copies + all_copies:
        copy.wait_send()
    for copy in first_copies:
        copy.wait_send()

    def drain_chain(k, carry):
        for yb in (0, 1):
            up_copy, down_copy, sib_copy = chain_copies(yb, k)

            @pl.when(goes_up[yb])
            def _():
                up_copy.wait_send()

            @pl.when(goes_down[yb])
            def _():
                down_copy.wait_send()

            sib_copy.wait_send()

        return carry

    lax.fori_loop(0, BLOCKS, drain_chain, 0)

    lax.fori_loop(0, PARTS + 1, spread_step, 0)

    def last_step(q, carry):
        for (rightward, to_right, to_left), v in zip(forwards(q), [zl] + line):
            to_right.wait_send()
        for copy in own_sends(q) + line_sends(q):
            copy.wait_send()
        for (rightward, to_right, to_left), v in zip(forwards(q), [zl] + line):
            out_arrived(q, v * NX + jnp.where(rightward, xr, xl))
            out_arrived(q, v * NX + xo)
        return carry

    lax.fori_loop(0, PARTS, last_step, 0)


def place_kernel(wide, moment, curv, wide_out, moment_out, curv_out, sem):
    copies = [
        pltpu.make_async_copy(
            wide.at[n], wide_out.at[:, pl.ds(n * COLS, COLS)], sem.at[n]
        )
        for n in range(NX * NL)
    ]
    copies.append(pltpu.make_async_copy(moment, moment_out, sem.at[NX * NL]))
    copies.append(pltpu.make_async_copy(curv, curv_out, sem.at[NX * NL + 1]))
    for copy in copies:
        copy.start()
    for copy in copies:
        copy.wait()


def on_device(
    gate_up, cot_mean, label_rows, true_labels, sampled_labels, weight, moment, curvature, bits
):
    dma = pltpu.SemaphoreType.DMA
    groups = NX * NL
    anywhere = pl.BlockSpec(memory_space=pl.ANY)
    in_hbm = pl.BlockSpec(memory_space=pltpu.HBM)
    in_vmem = pl.BlockSpec(memory_space=pltpu.VMEM)
    state = (ROWS, COLS)
    pieces, new_moment, new_curv = pl.pallas_call(
        step_kernel,
        out_shape=[
            pltpu.VMEM((groups, ROWS, COLS), BF16),
            pltpu.VMEM(state, BF16),
            pltpu.VMEM(state, BF16),
        ],
        in_specs=[in_hbm] * 9,
        out_specs=[in_vmem] * 3,
        scratch_shapes=[
            pltpu.VMEM((2, ROWS, TOK), BF16),
            pltpu.VMEM((TOK, HALF), BF16),
            pltpu.VMEM((CAND, COLS), BF16),
            pltpu.VMEM((1, TOK), I32),
            pltpu.VMEM((1, TOK), I32),
            pltpu.VMEM(state, BF16),
            pltpu.VMEM(state, BF16),
            pltpu.VMEM(state, BF16),
            pltpu.VMEM(state, I32),
            pltpu.VMEM((NL, ROWS, TOK), BF16),
            pltpu.VMEM((NX, NC, NL, TOK, HALF), BF16),
            pltpu.VMEM((NX, ROWS, COLS), BF16),
            pltpu.VMEM(state, F32),
            pltpu.VMEM((2, TOP, COLS), BF16),
            pltpu.VMEM((2, ROWS, COLS), BF16),
            pltpu.VMEM((NL, STEP, 2 * CAND), BF16),
            pltpu.VMEM((NL, STEP, 2 * CAND), BF16),
            pltpu.VMEM((NX, STEP, 2 * CAND), F32),
            pltpu.VMEM((NL, STEP, 2 * CAND), F32),
            pltpu.VMEM((2 * CAND, 2 * COLS), BF16),
            pltpu.VMEM((ROWS, 2 * COLS), F32),
            dma((9,)),
            dma((2, NH, SUB)),
            dma((2, NZ, SUB)),
            dma((2, BLOCKS, 2)),
            dma((2, BLOCKS)),
            dma((2, BLOCKS)),
            dma((NL - 1,)),
            dma((NL,)),
            dma((NL - 1,)),
            dma((NL,)),
            dma((NX - 1,)),
            dma((NX,)),
            dma((NL - 1,)),
            dma((NL,)),
            dma((2,)),
            dma((2,)),
            dma((2, PARTS)),
            dma((2, PARTS)),
            dma((PARTS, 15)),
            dma((PARTS, groups)),
        ],
        compiler_params=pltpu.CompilerParams(
            collective_id=0, has_side_effects=True, vmem_limit_bytes=58 * 1024 * 1024
        ),
        cost_estimate=pl.CostEstimate(
            flops=1_000_000_000, bytes_accessed=6_000_000, transcendentals=114_688
        ),
        name="sophia_step",
    )(
        jnp.swapaxes(gate_up, 1, 2), cot_mean, label_rows,
        true_labels.reshape(1, TOK), sampled_labels.reshape(1, TOK),
        weight, moment, curvature, bits,
    )
    return pl.pallas_call(
        place_kernel,
        out_shape=[
            jax.ShapeDtypeStruct((ROWS, groups * COLS), BF16),
            jax.ShapeDtypeStruct(state, BF16),
            jax.ShapeDtypeStruct(state, BF16),
        ],
        in_specs=[anywhere] * 3,
        out_specs=[in_hbm] * 3,
        scratch_shapes=[dma((groups + 2,))],
        compiler_params=pltpu.CompilerParams(vmem_limit_bytes=1024 * 1024),
        name="place",
    )(pieces, new_moment, new_curv)


def solution(mesh):
    in_specs = (
        P(None, "dp", "zero"),
        P("dp", "zero"),
        P(None, "dp"),
        P("dp"),
        P("dp"),
        P("zero", "dp"),
        P("zero", "dp"),
        P("zero", "dp"),
        P("zero", "dp"),
    )
    out_specs = (P("zero", None), P("zero", "dp"), P("zero", "dp"))
    return jax.shard_map(
        on_device, mesh=mesh, in_specs=in_specs, out_specs=out_specs, check_vma=False
    )
```
